32 devices in a mesh: groups: 1, node: 8 (over z, y), local: 4 (over x, core).
Axes of the slice: x: 2, y: 2, z: 4, core: 2. Of those that a mesh axis runs over, the one named last changes fastest.
Arguments:
- tokens: bfloat16 [4096, 2048], P(('groups', 'node', 'local')), may hold values from -6 to 6
- out_grad: bfloat16 [4096, 2048], P(('groups', 'node', 'local')), may hold values from -6 to 6
- routes: int32 [4096, 6], P(('groups', 'node', 'local')), may hold values from 0 to 15, all different within a row; in each aligned block of 128 rows (0 to 127, 128 to 255, ...) at most 72 rows name the same one
- route_weight: float32 [4096, 6], P(('groups', 'node', 'local')), may hold values from 0.02 to 0.4
- example_id: int32 [4096], P(('groups', 'node', 'local')), may hold values from 0 to 7, never falling along the last dimension, each value on 1 to 1024 neighbouring positions
- gate_weight: bfloat16 [32, 2048, 704], P(('node', 'local')), may hold values from -0.125 to 0.125
- up_weight: bfloat16 [32, 2048, 704], P(('node', 'local')), may hold values from -0.125 to 0.125
- hidden_basis: bfloat16 [32, 704, 64], P(('node', 'local')), may hold values from -0.15625 to 0.15625
- model_basis: bfloat16 [32, 1024, 64], P(('node', 'local')), may hold values from -0.125 to 0.125
Outputs:
- logged: float32 [16, 8, 64, 64], P('node', ('groups', 'local'))
The draws below stay inside these ranges and needn't reach their ends.
Inputs may be any that keep to these rules, and one draw needn't show every extreme that they name: `routes`: each token names 6 different experts. Within the 128 tokens of one device (aligned blocks), no expert is named more than 72 times, a bound that some block reaches. `example_id`: never falls along the tokens; each example holds 1 to 1024 tokens.
All inputs are finite; a program needn't handle non-finite values.
Results may differ from the reference program's by a relative error of at most 0.0041.
Values may be sent and summed in bfloat16 or wider, within the bound.
A program may use at most 128 MiB of HBM per device.

```python
import math
import jax
import jax.numpy as jnp
import numpy as np
from jax import lax

D = 2048
H = 1408
TOP = 6
RANK = 64
TOK_DEV = 128
HALF = 704
EXPERTS = 16
SLOTS = 32
TOKENS = 4096
CAP = 72
EXAMPLES = 8
N_NODE = 8
N_LOCAL = 4


def steps_of(rng, dims, split, low, top_value):
    def one(dim, blocks):
        heights = jax.random.uniform(jax.random.fold_in(jax.random.fold_in(rng, 6), dim), (blocks,), jnp.float32, low / len(split), top_value / len(split))
        return jnp.repeat(jnp.exp(heights), dims[dim] // blocks).reshape((-1,) + (1,) * (len(dims) - dim - 1))

    gain = one(*split[0])
    for cut in split[1:]:
        gain = gain * one(*cut)
    return gain


def length_profile(number_of, total, reach, slope):
    loads = [(1 << 20) // math.isqrt(rank ** slope) + 1 for rank in range(2, number_of + 1)]
    surplus, holding = total - reach - (number_of - 1), [1] * (number_of - 1)
    while surplus > 0:
        free = [i for i in range(number_of - 1) if holding[i] < reach]
        whole, budget = sum([loads[i] for i in free]), surplus
        for i in free:
            addition = min(reach - holding[i], max(1, budget * loads[i] // whole), surplus)
            holding[i] = holding[i] + addition
            surplus = surplus - addition
    return np.array([reach] + holding)


def uneven_parts(rng, count, total, reach, slope):
    if count == 2:
        one = jax.random.randint(rng, (), max(1, total - reach), min(reach, total - 1) + 1)
        return jnp.stack([one, total - one])
    lengths = jnp.asarray(length_profile(count, total, reach, slope), jnp.int32)
    couples = (count - 1) // 2
    giver, receiver = lengths[1:1 + 2 * couples:2], lengths[2:2 + 2 * couples:2]
    room = jnp.minimum(giver - 1, reach - receiver)
    moved = jax.random.randint(jax.random.fold_in(rng, 1), (couples,), 0, 1 << 20) % (room + 1)
    lengths = lengths.at[1:1 + 2 * couples:2].set(giver - moved).at[2:2 + 2 * couples:2].set(receiver + moved)
    return lengths[jax.random.permutation(jax.random.fold_in(rng, 2), count)]


def deal_out(rng, own, number, rows, amount, top, bound, skew):
    ranking = jax.random.permutation(rng, amount)
    heavy_load, usual = load_shares(amount, rows * top, bound, skew, True), load_shares(amount, rows * top, bound, skew, False)
    places = jnp.arange(amount)

    def named(tallies, rotation):
        used = int((tallies > 0).sum())
        fixed = max(1, used // 4)
        shifted = fixed + (places - fixed + rotation * (used - fixed)) % max(1, amount - fixed)
        return jnp.zeros((amount,), jnp.int32).at[ranking[jnp.where(places < fixed, places, shifted)]].set(jnp.asarray(tallies, jnp.int32))

    tallies = jnp.where(number % 4 == 0, named(heavy_load, number // 4), named(usual, number - number // 4 - 1))
    mixed = jax.random.permutation(jax.random.fold_in(own, 3), amount)
    source_of, receiver = mixed[0:amount // 2 * 2:2], mixed[1:amount // 2 * 2:2]
    room = jnp.minimum(tallies[source_of] - 1, bound - tallies[receiver]) // 2
    room = jnp.where((source_of == ranking[0]) | (receiver == ranking[0]) | (tallies[receiver] == 0), 0, jnp.maximum(room, 0))
    shifted = jax.random.randint(jax.random.fold_in(own, 4), (amount // 2,), 0, 1 << 20) % (room + 1)
    tallies = tallies.at[source_of].add(-shifted).at[receiver].add(shifted)
    members = jnp.searchsorted(jnp.cumsum(tallies), jnp.arange(rows * top), side="right").astype(jnp.int32)
    grid = members.reshape(top, rows).T
    grid = grid[jax.random.permutation(jax.random.fold_in(own, 1), rows)]
    rotation = jax.random.randint(jax.random.fold_in(own, 2), (rows, 1), 0, top)
    return jnp.take_along_axis(grid, (jnp.arange(top)[None, :] + rotation) % top, axis=1)


def load_shares(number_of, total, reach, skew, full):
    portions = [(1 << 20) // math.isqrt(standing ** skew) + 1 for standing in range(1, number_of + 1)]
    largest = reach if full else min(reach, max(-(-total // number_of), total * portions[0] // sum(portions)))
    least = 1 if total - largest >= number_of - 1 else 0
    given, rest = [largest] + [least] * (number_of - 1), total - largest - least * (number_of - 1)
    while rest > 0:
        candidates = [i for i in range(1, number_of) if given[i] < largest] or [i for i in range(1, number_of) if given[i] < reach]
        pool, left = sum([portions[i] for i in candidates]), rest
        for i in candidates:
            more = min(reach - given[i], max(1, left * portions[i] // pool), rest)
            given[i] = given[i] + more
            rest = rest - more
    return np.array(given)


def gaussian(own_key, shape, width, limit, shards=(), kind=jnp.bfloat16):
    drawn = width * jax.random.normal(own_key, shape, jnp.float32)
    if shards:
        drawn = drawn * steps_of(own_key, shape, shards, -0.22, 0.18)
    return jnp.clip(drawn, -limit, limit).astype(kind)


def setup_inputs(seed: int = 0, part: int = 0) -> dict:
    splits = jax.random.split(jax.random.key(seed), 10)
    part_splits = jax.random.split(jax.random.fold_in(splits[9], part), 10)
    tokens = gaussian(part_splits[0], (TOKENS, D), 1.0, 6.0, ((0, 32),))
    out_grad = gaussian(part_splits[1], (TOKENS, D), 1.0, 6.0, ((0, 32),))
    routes_keys = jax.random.split(jax.random.fold_in(part_splits[2], 1), TOKENS // TOK_DEV)
    routes_turns = jax.random.permutation(jax.random.fold_in(part_splits[2], 3), TOKENS // TOK_DEV)
    routes = jax.vmap(lambda own, number: deal_out(jax.random.fold_in(part_splits[2], 2), own, number, TOK_DEV, EXPERTS, TOP, CAP, 2))(routes_keys, routes_turns).reshape((TOKENS, TOP))
    route_weight = jnp.clip(0.02 + 0.38 * jax.random.uniform(part_splits[3], (TOKENS, TOP), jnp.float32) ** steps_of(part_splits[3], (TOKENS, TOP), ((0, 32),), -0.2, 0.2), 0.02, 0.4)
    example_id = jnp.searchsorted(jnp.cumsum(uneven_parts(part_splits[4], EXAMPLES, TOKENS, 2 * TOKENS // EXAMPLES, 2)), jnp.arange(TOKENS), side="right").astype(jnp.int32)
    gate_weight = gaussian(splits[5], (SLOTS, D, HALF), D ** -0.5, 0.125, ((0, 32),))
    up_weight = gaussian(splits[6], (SLOTS, D, HALF), D ** -0.5, 0.125, ((0, 32),))
    hidden_basis = gaussian(splits[7], (SLOTS, HALF, RANK), H ** -0.5, 0.15625, ((0, 32),))
    model_basis = gaussian(splits[8], (SLOTS, D // 2, RANK), D ** -0.5, 0.125, ((0, 32),))
    return dict(tokens=tokens, out_grad=out_grad, routes=routes, route_weight=route_weight, example_id=example_id, gate_weight=gate_weight, up_weight=up_weight, hidden_basis=hidden_basis, model_basis=model_basis)


def reference(tokens, out_grad, routes, route_weight, example_id, gate_weight, up_weight, hidden_basis, model_basis):
    flat_routes = routes.reshape(-1)
    flat_weight = route_weight.reshape(-1)
    row_bound = N_NODE * N_LOCAL * CAP
    example_ids = jnp.arange(EXAMPLES, dtype=jnp.int32)

    def one_expert(expert):
        is_routed = flat_routes == expert
        routed_count = jnp.sum(is_routed.astype(jnp.int32))
        positions = jnp.nonzero(is_routed, size=row_bound, fill_value=0)[0].astype(jnp.int32)
        in_use = jnp.arange(row_bound, dtype=jnp.int32) < routed_count
        token_of = positions // TOP
        weight = jnp.where(in_use, flat_weight[positions], jnp.zeros((), flat_weight.dtype))
        features = tokens[token_of]
        scaled = (weight[:, None] * out_grad[token_of].astype(jnp.float32)).astype(jnp.bfloat16)
        gate_full = jnp.concatenate([gate_weight[2 * expert], gate_weight[2 * expert + 1]], axis=1)
        up_full = jnp.concatenate([up_weight[2 * expert], up_weight[2 * expert + 1]], axis=1)
        hidden_full = jnp.concatenate([hidden_basis[2 * expert], hidden_basis[2 * expert + 1]], axis=0)
        model_full = jnp.concatenate([model_basis[2 * expert], model_basis[2 * expert + 1]], axis=0)
        gate_pre = jnp.dot(features, gate_full, preferred_element_type=jnp.float32)
        up_pre = jnp.dot(features, up_full, preferred_element_type=jnp.float32)
        hidden = (jax.nn.silu(gate_pre) * up_pre).astype(jnp.bfloat16)
        left_side = jnp.dot(hidden, hidden_full, preferred_element_type=jnp.float32)
        right_side = jnp.dot(scaled, model_full, preferred_element_type=jnp.float32)
        member = (example_id[token_of][:, None] == example_ids[None, :]).astype(jnp.float32)
        return jnp.einsum("re,ra,rb->eab", member, left_side, right_side, precision=lax.Precision.HIGHEST)

    return lax.map(one_expert, jnp.arange(EXPERTS, dtype=jnp.int32))
```

```python
import functools

import jax
import jax.numpy as jnp
from jax import lax
from jax.experimental import pallas as pl
from jax.experimental.pallas import tpu as pltpu
from jax.sharding import PartitionSpec as P

MESH = pl.DeviceIdType.MESH


def swapped(block, axis, stride):
    count = lax.axis_size(axis)
    route = []
    for low in range(count):
        high = low | 1 << stride
        if high != low and high < count:
            route += [(low, high), (high, low)]
    return lax.ppermute(block, axis, route)


def local(
    tokens,
    out_grad,
    routes,
    route_weight,
    example_id,
    gate_weight,
    up_weight,
    hidden_basis,
    model_basis,
):
    node_count = lax.axis_size("node")
    local_count = lax.axis_size("local")
    experts = node_count * local_count // 2
    per_node = local_count // 2
    tok_rows, model_width = tokens.shape
    top_count = routes.shape[1]
    capacity = 3 * tok_rows * top_count // (2 * experts)
    half_width = model_width // 2
    examples = 2 * local_count
    rank_size = hidden_basis.shape[2]
    flat_routes = routes.reshape(-1)
    expert_ids = jnp.arange(experts, dtype=jnp.int32)
    chosen = (flat_routes[:, None] == expert_ids[None, :]).astype(jnp.int32)
    earlier = jnp.cumsum(chosen, axis=0) - chosen
    placing = jnp.sum(earlier * chosen, axis=1)
    target = flat_routes * capacity + placing
    owner_row = (
        jnp.full((experts * capacity,), -1, jnp.int32)
        .at[target]
        .set(jnp.arange(tok_rows * top_count, dtype=jnp.int32))
    )
    filled = owner_row >= 0
    source = jnp.maximum(owner_row, 0)
    token_of = source // top_count
    weight_of = jnp.where(filled, route_weight.reshape(-1)[source], jnp.zeros((), jnp.float32))
    sent_rows = jnp.where(filled[:, None], tokens[token_of], jnp.zeros((), tokens.dtype))
    sent_grads = (weight_of[:, None] * out_grad[token_of].astype(jnp.float32)).astype(jnp.bfloat16)
    sent_examples = example_id[token_of].astype(jnp.bfloat16)
    grid_feats = jnp.repeat(sent_rows.reshape(experts, capacity, model_width), 2, axis=0)
    grid_grads = (
        sent_grads.reshape(experts, capacity, 2, half_width)
        .transpose(0, 2, 1, 3)
        .reshape(2 * experts, capacity, half_width)
    )
    grid_examples = jnp.repeat(sent_examples.reshape(experts, capacity), 2, axis=0)
    row_feats = lax.all_to_all(
        grid_feats, ("node", "local"), split_axis=0, concat_axis=0, tiled=True
    )
    row_grads = lax.all_to_all(
        grid_grads, ("node", "local"), split_axis=0, concat_axis=0, tiled=True
    )
    row_examples = lax.all_to_all(
        grid_examples, ("node", "local"), split_axis=0, concat_axis=0, tiled=True
    )
    leading = row_feats.shape[:2]
    flat_feats = row_feats.reshape(-1, model_width)
    gate_proj = jnp.dot(flat_feats, gate_weight[0], preferred_element_type=jnp.float32)
    up_proj = jnp.dot(flat_feats, up_weight[0], preferred_element_type=jnp.float32)
    hidden = (jax.nn.silu(gate_proj) * up_proj).astype(jnp.bfloat16)
    left_side = jnp.dot(hidden, hidden_basis[0], preferred_element_type=jnp.float32)
    right_part = jnp.dot(
        row_grads.reshape(-1, half_width), model_basis[0], preferred_element_type=jnp.float32
    )
    left_side, right_part, arrived = (
        left_side.reshape(leading + (rank_size,)),
        right_part.reshape(leading + (rank_size,)),
        row_examples,
    )
    right_side = right_part + swapped(right_part, "local", 0)
    flat_left = left_side.reshape(-1, rank_size)
    flat_right = right_side.reshape(-1, rank_size)
    flat_examples = arrived.reshape(-1).astype(jnp.int32)
    member = (flat_examples[:, None] == jnp.arange(examples, dtype=jnp.int32)[None, :]).astype(
        jnp.float32
    )
    spread = (member[:, :, None] * flat_left[:, None, :]).reshape(
        flat_left.shape[0], examples * rank_size
    )
    logged_own = lax.dot_general(
        spread,
        flat_right,
        (((0,), (0,)), ((), ())),
        precision=lax.Precision.HIGHEST,
        preferred_element_type=jnp.float32,
    ).reshape(examples, rank_size, rank_size)
    slot_in_node = lax.axis_index("local") // 2
    chooser = (jnp.arange(per_node, dtype=jnp.int32) == slot_in_node).astype(jnp.float32)
    padded_term = chooser[:, None, None, None] * logged_own[None]
    return lax.psum_scatter(padded_term, "local", scatter_dimension=1, tiled=True)


def fused_kernel(
    tok_ref,
    grad_ref,
    coef_ref,
    aux_ref,
    gate_ref,
    up_ref,
    hid_ref,
    basis_ref,
    out_ref,
    tbuf,
    qbuf,
    rmsg,
    rbuf,
    lbuf,
    acc,
    fsend,
    fbuf,
    own_sem,
    t_send,
    t_recv,
    ts_recv,
    q_send,
    q_recv,
    qs_recv,
    r_send,
    r_recv,
    rs_sem,
    f_send,
    f_recv,
):
    group = lax.axis_index("groups")
    node = lax.axis_index("node")
    spot = lax.axis_index("local")
    depth = lax.axis_size("node") // 2
    chips = 2 * lax.axis_size("node")
    pairs = lax.axis_size("local")
    zi, yi = node // 2, node % 2
    xi, core = spot // 2, spot % 2
    me = node * 2 + xi
    half = grad_ref.shape[1] // 2
    rank = hid_ref.shape[0]
    rows = tok_ref.shape[0]

    def device(z, y, x, c):
        return (group, z * 2 + y, x * 2 + c)

    first_x, first_y = 1 - core, core
    up = device(lax.rem(zi + 1, depth), yi, xi, core)
    down = device(lax.rem(zi + depth - 1, depth), yi, xi, core)
    near = device(zi, (yi + first_y) % 2, (xi + first_x) % 2, core)
    far = device(zi, (yi + first_x) % 2, (xi + first_y) % 2, core)
    twin = device(zi, yi, xi, 1 - core)

    barrier = pltpu.get_barrier_semaphore()

    @pl.loop(1, chips)
    def _(step):
        chip = (me + step) % chips
        pl.semaphore_signal(
            barrier, inc=1, device_id=(group, chip // 2, (chip % 2) * 2 + core), device_id_type=MESH
        )

    for c in (0, 1):
        where = device(zi, yi, (xi + c) % 2, 1 - core)
        pl.semaphore_signal(barrier, inc=1, device_id=where, device_id_type=MESH)
    pl.semaphore_wait(barrier, chips + 1)

    def place(idx):
        k, pos = idx // 4, idx % 4
        one, two = pos % 2, pos // 2
        away = (k + 1) // 2
        dz = away * (1 - 2 * (k % 2))
        oz = zi + dz
        valid = (oz >= 0) & (oz < depth)
        oz = jnp.clip(oz, 0, depth - 1)
        flip_x = one * first_x + two * first_y
        flip_y = one * first_y + two * first_x
        origin = (oz * 2 + (yi + flip_y) % 2) * 2 + (xi + flip_x) % 2
        return origin, valid, one, two, dz

    def links(idx, view, send, recv, twin_recv):
        origin, valid, one, two, dz = place(idx)
        straight = valid & (one == 0) & (two == 0)
        plan = (
            (straight & (dz <= 0) & (zi < depth - 1), up, recv),
            (straight & (dz >= 0) & (zi > 0), down, recv),
            (valid & (two == 0), far, recv),
            (straight, near, recv),
            (valid, twin, twin_recv),
        )
        for j, (wanted, where, sem) in enumerate(plan):
            copy = pltpu.make_async_remote_copy(
                src_ref=view(origin, core),
                dst_ref=view(origin, core),
                send_sem=send.at[origin, j],
                recv_sem=sem.at[origin],
                device_id=where,
                device_id_type=MESH,
            )
            yield wanted, copy

    def arrival(view, origin, c, send, sem):
        return pltpu.make_async_remote_copy(
            src_ref=view(origin, c),
            dst_ref=view(origin, c),
            send_sem=send.at[0, 0],
            recv_sem=sem.at[origin],
            device_id=twin,
            device_id_type=MESH,
        )

    def forward(idx, view, send, recv, twin_recv):
        origin, valid, *_ = place(idx)

        @pl.when(valid & (idx > 0))
        def _():
            arrival(view, origin, core, send, recv).wait_recv()

        for wanted, copy in links(idx, view, send, recv, twin_recv):
            pl.when(wanted)(copy.start)

    def finish(idx, view, send, recv, twin_recv):
        for wanted, copy in links(idx, view, send, recv, twin_recv):
            pl.when(wanted)(copy.wait_send)

    def t_view(origin, c):
        return tbuf.at[origin, c]

    def q_view(origin, c):
        return qbuf.at[c, origin]

    t_all = (t_view, t_send, t_recv, ts_recv)
    q_all = (q_view, q_send, q_recv, qs_recv)
    positions = 4 * (2 * depth - 1)

    own_q = pltpu.make_async_copy(basis_ref, qbuf.at[core, me], own_sem.at[0])
    own_t = pltpu.make_async_copy(tok_ref, tbuf.at[me, core], own_sem.at[1])
    own_q.start()
    own_t.start()
    own_q.wait()

    @pl.loop(0, positions)
    def _(idx):
        forward(idx, *q_all)

    own_t.wait()
    forward(0, *t_all)

    @pl.loop(0, chips)
    def _(chip):
        arrival(q_view, chip, 1 - core, q_send, qs_recv).wait_recv()

    @pl.loop(0, chips)
    def _(chip):
        total = None
        for h in (0, 1):
            block = qbuf[h, chip]
            twice = jnp.concatenate([block, block], axis=0)
            term = lax.dot_general(
                grad_ref[:, h * half : (h + 1) * half],
                twice,
                (((1,), (1,)), ((), ())),
                preferred_element_type=jnp.float32,
            )
            total = term if total is None else total + term
        lanes = lax.broadcasted_iota(jnp.int32, coef_ref.shape, 1)
        column = jnp.sum(jnp.where(lanes == chip, coef_ref[...], 0.0), axis=1, keepdims=True)
        rmsg[chip, :rows] = (total * column).astype(jnp.bfloat16)
        rmsg[chip, rows:] = aux_ref[...]

    def r_copy(chip):
        return pltpu.make_async_remote_copy(
            src_ref=rmsg.at[chip],
            dst_ref=rbuf.at[core, me],
            send_sem=r_send.at[chip],
            recv_sem=r_recv.at[me],
            device_id=(group, chip // 2, (chip % 2) * 2 + core),
            device_id_type=MESH,
        )

    own_r = pltpu.make_async_copy(rmsg.at[me], rbuf.at[core, me], own_sem.at[2])
    own_r.start()

    @pl.loop(1, chips)
    def _(step):
        r_copy((me + step) % chips).start()

    def compute(origin):
        feats = tbuf[origin].reshape(2 * rows, tok_ref.shape[1])
        gate = jnp.dot(feats, gate_ref[...], preferred_element_type=jnp.float32)
        upper = jnp.dot(feats, up_ref[...], preferred_element_type=jnp.float32)
        hidden = (gate / (1.0 + jnp.exp(-gate)) * upper).astype(jnp.bfloat16)
        left = lax.dot_general(
            hid_ref[...],
            hidden,
            (((1,), (1,)), ((), ())),
            preferred_element_type=jnp.float32,
        )
        high = left.astype(jnp.bfloat16)
        low = (left - high.astype(jnp.float32)).astype(jnp.bfloat16)
        lbuf[origin, :rank] = high
        lbuf[origin, rank:] = low

    lag = 2

    @pl.loop(0, positions + lag)
    def _(idx):
        @pl.when((idx > 0) & (idx < positions))
        def _():
            forward(idx, *t_all)

        earlier = jnp.maximum(idx - lag, 0)
        origin, valid, *_ = place(earlier)

        @pl.when(valid & (idx >= lag))
        def _():
            arrival(t_view, origin, 1 - core, t_send, ts_recv).wait_recv()
            compute(origin)

    own_r.wait()

    @pl.loop(1, chips)
    def _(step):
        chip = (me + step) % chips
        pltpu.make_async_remote_copy(
            src_ref=rmsg.at[chip],
            dst_ref=rbuf.at[core, chip],
            send_sem=r_send.at[chip],
            recv_sem=r_recv.at[chip],
            device_id=twin,
            device_id_type=MESH,
        ).wait_recv()

    share = pltpu.make_async_remote_copy(
        src_ref=rbuf.at[core],
        dst_ref=rbuf.at[core],
        send_sem=rs_sem.at[0],
        recv_sem=rs_sem.at[1],
        device_id=twin,
        device_id_type=MESH,
    )
    share.start()
    share.wait_recv()

    acc[...] = jnp.zeros_like(acc)

    @pl.loop(0, chips)
    def _(chip):
        token = lax.broadcasted_iota(jnp.int32, (rows, 2 * rank), 0).astype(jnp.float32)
        parts = []
        for c in (0, 1):
            right = rbuf[c, chip, :rows].astype(jnp.float32)
            bounds = rbuf[c, chip, rows:].astype(jnp.float32)
            cols = []
            for p in range(pairs):
                inside = (token >= bounds[p : p + 1]) & (token < bounds[pairs + p : pairs + p + 1])
                cols.append(jnp.where(inside, right, 0.0).astype(jnp.bfloat16))
            parts.append(jnp.concatenate(cols, axis=1))
        spread = jnp.concatenate(parts, axis=0)
        acc[...] += jnp.dot(lbuf[chip], spread, preferred_element_type=jnp.float32)

    width = 2 * rank
    for p in range(pairs):
        cut = slice(p * width, (p + 1) * width)
        fsend[p] = acc[:rank, cut] + acc[rank:, cut]
    fbuf[spot] = fsend[spot]

    def f_copy(step, source):
        peer = (spot + step) % pairs
        return pltpu.make_async_remote_copy(
            src_ref=fsend.at[peer],
            dst_ref=fbuf.at[peer if source else spot],
            send_sem=f_send.at[peer],
            recv_sem=f_recv.at[peer if source else spot],
            device_id=(group, node, peer),
            device_id_type=MESH,
        )

    for step in range(1, pairs):
        f_copy(step, False).start()
    for step in range(1, pairs):
        f_copy(step, True).wait_recv()
    for e in range(pairs // 2):
        out_ref[e] = fbuf[2 * e] + fbuf[2 * e + 1]

    for step in range(1, pairs):
        f_copy(step, False).wait_send()
    share.wait_send()

    @pl.loop(1, chips)
    def _(step):
        r_copy((me + step) % chips).wait_send()

    @pl.loop(0, positions)
    def _(idx):
        finish(idx, *q_all)
        finish(idx, *t_all)


def fused_local(
    tokens,
    out_grad,
    routes,
    route_weight,
    example_id,
    gate_weight,
    up_weight,
    hidden_basis,
    model_basis,
):
    local_count = lax.axis_size("local")
    chips = lax.axis_size("node") * local_count // 2
    examples = 2 * local_count
    rows, width = tokens.shape
    half_width = hidden_basis.shape[1]
    rank = hidden_basis.shape[2]
    chosen = routes[:, :, None] == jnp.arange(chips, dtype=jnp.int32)
    coef = jnp.sum(jnp.where(chosen, route_weight[:, :, None], 0.0), axis=1)
    before = jnp.sum(
        example_id[None, :] < jnp.arange(examples + 1, dtype=jnp.int32)[:, None], axis=1
    )
    low = jnp.repeat(before[:-1], rank).reshape(local_count, 2 * rank)
    high = jnp.repeat(before[1:], rank).reshape(local_count, 2 * rank)
    fill = jnp.zeros((16 - 2 * local_count, 2 * rank), low.dtype)
    aux = jnp.concatenate([low, high, fill]).astype(jnp.bfloat16)
    vmem = pl.BlockSpec(memory_space=pltpu.VMEM)
    dma = pltpu.SemaphoreType.DMA
    bf16, f32 = jnp.bfloat16, jnp.float32
    flops = 2 * 2 * rows * chips * width * 2 * half_width
    logged = pl.pallas_call(
        fused_kernel,
        out_shape=jax.ShapeDtypeStruct((local_count // 2, rank, 2 * rank), f32),
        in_specs=[vmem] * 8,
        out_specs=vmem,
        scratch_shapes=[
            pltpu.VMEM((chips, 2, rows, width), bf16),
            pltpu.VMEM((2, chips, rank, width // 2), bf16),
            pltpu.VMEM((chips, rows + 16, 2 * rank), bf16),
            pltpu.VMEM((2, chips, rows + 16, 2 * rank), bf16),
            pltpu.VMEM((chips, 2 * rank, 2 * rows), bf16),
            pltpu.VMEM((2 * rank, examples * rank), f32),
            pltpu.VMEM((local_count, rank, 2 * rank), f32),
            pltpu.VMEM((local_count, rank, 2 * rank), f32),
            dma((3,)),
            dma((chips, 5)),
            dma((chips,)),
            dma((chips,)),
            dma((chips, 5)),
            dma((chips,)),
            dma((chips,)),
            dma((chips,)),
            dma((chips,)),
            dma((2,)),
            dma((local_count,)),
            dma((local_count,)),
        ],
        compiler_params=pltpu.CompilerParams(
            collective_id=0, has_side_effects=True, vmem_limit_bytes=56 * 1024 * 1024
        ),
        cost_estimate=pl.CostEstimate(flops=flops, bytes_accessed=1 << 23, transcendentals=0),
    )(
        tokens,
        out_grad,
        coef,
        aux,
        gate_weight[0],
        up_weight[0],
        hidden_basis[0].T,
        model_basis[0].T,
    )
    logged = logged.reshape(local_count // 2, rank, 2, rank)
    return logged.transpose(0, 2, 1, 3)


def solution(mesh):
    sizes = dict(mesh.shape)
    small = sizes["node"] == 8 and sizes["local"] == 4
    body = fused_local if small else local
    in_specs = (
        P(("groups", "node", "local"), None),
        P(("groups", "node", "local"), None),
        P(("groups", "node", "local"), None),
        P(("groups", "node", "local"), None),
        P(("groups", "node", "local")),
        P(("node", "local"), None, None),
        P(("node", "local"), None, None),
        P(("node", "local"), None, None),
        P(("node", "local"), None, None),
    )
    out_specs = P("node", ("groups", "local"), None, None)
    return jax.shard_map(body, mesh=mesh, in_specs=in_specs, out_specs=out_specs, check_vma=False)
```

```python
import functools

import jax
import jax.numpy as jnp
from jax import lax
from jax.experimental import pallas as pl
from jax.experimental.pallas import tpu as pltpu
from jax.sharding import PartitionSpec as P

MESH = pl.DeviceIdType.MESH


def swapped(block, axis, stride):
    count = lax.axis_size(axis)
    route = []
    for low in range(count):
        high = low | 1 << stride
        if high != low and high < count:
            route += [(low, high), (high, low)]
    return lax.ppermute(block, axis, route)


def local(
    tokens,
    out_grad,
    routes,
    route_weight,
    example_id,
    gate_weight,
    up_weight,
    hidden_basis,
    model_basis,
):
    node_count = lax.axis_size("node")
    local_count = lax.axis_size("local")
    experts = node_count * local_count // 2
    per_node = local_count // 2
    tok_rows, model_width = tokens.shape
    top_count = routes.shape[1]
    capacity = 3 * tok_rows * top_count // (2 * experts)
    half_width = model_width // 2
    examples = 2 * local_count
    rank_size = hidden_basis.shape[2]
    flat_routes = routes.reshape(-1)
    expert_ids = jnp.arange(experts, dtype=jnp.int32)
    chosen = (flat_routes[:, None] == expert_ids[None, :]).astype(jnp.int32)
    earlier = jnp.cumsum(chosen, axis=0) - chosen
    placing = jnp.sum(earlier * chosen, axis=1)
    target = flat_routes * capacity + placing
    owner_row = (
        jnp.full((experts * capacity,), -1, jnp.int32)
        .at[target]
        .set(jnp.arange(tok_rows * top_count, dtype=jnp.int32))
    )
    filled = owner_row >= 0
    source = jnp.maximum(owner_row, 0)
    token_of = source // top_count
    weight_of = jnp.where(filled, route_weight.reshape(-1)[source], jnp.zeros((), jnp.float32))
    sent_rows = jnp.where(filled[:, None], tokens[token_of], jnp.zeros((), tokens.dtype))
    sent_grads = (weight_of[:, None] * out_grad[token_of].astype(jnp.float32)).astype(jnp.bfloat16)
    sent_examples = example_id[token_of].astype(jnp.bfloat16)
    grid_feats = jnp.repeat(sent_rows.reshape(experts, capacity, model_width), 2, axis=0)
    grid_grads = (
        sent_grads.reshape(experts, capacity, 2, half_width)
        .transpose(0, 2, 1, 3)
        .reshape(2 * experts, capacity, half_width)
    )
    grid_examples = jnp.repeat(sent_examples.reshape(experts, capacity), 2, axis=0)
    row_feats = lax.all_to_all(
        grid_feats, ("node", "local"), split_axis=0, concat_axis=0, tiled=True
    )
    row_grads = lax.all_to_all(
        grid_grads, ("node", "local"), split_axis=0, concat_axis=0, tiled=True
    )
    row_examples = lax.all_to_all(
        grid_examples, ("node", "local"), split_axis=0, concat_axis=0, tiled=True
    )
    leading = row_feats.shape[:2]
    flat_feats = row_feats.reshape(-1, model_width)
    gate_proj = jnp.dot(flat_feats, gate_weight[0], preferred_element_type=jnp.float32)
    up_proj = jnp.dot(flat_feats, up_weight[0], preferred_element_type=jnp.float32)
    hidden = (jax.nn.silu(gate_proj) * up_proj).astype(jnp.bfloat16)
    left_side = jnp.dot(hidden, hidden_basis[0], preferred_element_type=jnp.float32)
    right_part = jnp.dot(
        row_grads.reshape(-1, half_width), model_basis[0], preferred_element_type=jnp.float32
    )
    left_side, right_part, arrived = (
        left_side.reshape(leading + (rank_size,)),
        right_part.reshape(leading + (rank_size,)),
        row_examples,
    )
    right_side = right_part + swapped(right_part, "local", 0)
    flat_left = left_side.reshape(-1, rank_size)
    flat_right = right_side.reshape(-1, rank_size)
    flat_examples = arrived.reshape(-1).astype(jnp.int32)
    member = (flat_examples[:, None] == jnp.arange(examples, dtype=jnp.int32)[None, :]).astype(
        jnp.float32
    )
    spread = (member[:, :, None] * flat_left[:, None, :]).reshape(
        flat_left.shape[0], examples * rank_size
    )
    logged_own = lax.dot_general(
        spread,
        flat_right,
        (((0,), (0,)), ((), ())),
        precision=lax.Precision.HIGHEST,
        preferred_element_type=jnp.float32,
    ).reshape(examples, rank_size, rank_size)
    slot_in_node = lax.axis_index("local") // 2
    chooser = (jnp.arange(per_node, dtype=jnp.int32) == slot_in_node).astype(jnp.float32)
    padded_term = chooser[:, None, None, None] * logged_own[None]
    return lax.psum_scatter(padded_term, "local", scatter_dimension=1, tiled=True)


def fused_kernel(
    tok_ref,
    grad_ref,
    route_ref,
    weight_ref,
    aux_ref,
    gate_ref,
    up_ref,
    hid_ref,
    basis_ref,
    out_ref,
    wbuf,
    tbuf,
    qbuf,
    rmsg,
    rbuf,
    lbuf,
    acc,
    fsend,
    fbuf,
    own_sem,
    t_send,
    t_recv,
    ts_recv,
    q_send,
    q_recv,
    qs_recv,
    r_send,
    r_recv,
    rs_sem,
    f_send,
    f_recv,
):
    group = lax.axis_index("groups")
    node = lax.axis_index("node")
    spot = lax.axis_index("local")
    depth = lax.axis_size("node") // 2
    chips = 2 * lax.axis_size("node")
    pairs = lax.axis_size("local")
    zi, yi = node // 2, node % 2
    xi, core = spot // 2, spot % 2
    me = node * 2 + xi
    half = grad_ref.shape[1] // 2
    rank = hid_ref.shape[0]
    rows = tok_ref.shape[0]

    def device(z, y, x, c):
        return (group, z * 2 + y, x * 2 + c)

    first_x, first_y = 1 - core, core
    up = device(lax.rem(zi + 1, depth), yi, xi, core)
    down = device(lax.rem(zi + depth - 1, depth), yi, xi, core)
    near = device(zi, (yi + first_y) % 2, (xi + first_x) % 2, core)
    far = device(zi, (yi + first_x) % 2, (xi + first_y) % 2, core)
    twin = device(zi, yi, xi, 1 - core)

    barrier = pltpu.get_barrier_semaphore()

    @pl.loop(1, chips)
    def _(step):
        chip = (me + step) % chips
        pl.semaphore_signal(
            barrier, inc=1, device_id=(group, chip // 2, (chip % 2) * 2 + core), device_id_type=MESH
        )

    for c in (0, 1):
        where = device(zi, yi, (xi + c) % 2, 1 - core)
        pl.semaphore_signal(barrier, inc=1, device_id=where, device_id_type=MESH)
    pl.semaphore_wait(barrier, chips + 1)

    least = jnp.minimum(zi, depth - 1 - zi)
    lean = jnp.where(zi > depth - 1 - zi, -1, 1)

    def place(idx):
        n, pos = idx // 4, idx % 4
        one, two = pos % 2, pos // 2
        swing = ((n + 1) // 2) * (1 - 2 * (n % 2))
        dz = jnp.where(n <= 2 * least, swing, lean * (n - least))
        oz = jnp.clip(zi + dz, 0, depth - 1)
        flip_x = one * first_x + two * first_y
        flip_y = one * first_y + two * first_x
        origin = (oz * 2 + (yi + flip_y) % 2) * 2 + (xi + flip_x) % 2
        return origin, one, two, dz

    def links(idx, view, send, recv, twin_recv):
        origin, one, two, dz = place(idx)
        straight = (one == 0) & (two == 0)
        plan = (
            (straight & (dz <= 0) & (zi < depth - 1), up, recv),
            (straight & (dz >= 0) & (zi > 0), down, recv),
            (two == 0, far, recv),
            (straight, near, recv),
            (None, twin, twin_recv),
        )
        for j, (wanted, where, sem) in enumerate(plan):
            copy = pltpu.make_async_remote_copy(
                src_ref=view(origin, core),
                dst_ref=view(origin, core),
                send_sem=send.at[origin, j],
                recv_sem=sem.at[origin],
                device_id=where,
                device_id_type=MESH,
            )
            yield wanted, copy

    def arrival(view, origin, c, send, sem):
        return pltpu.make_async_remote_copy(
            src_ref=view(origin, c),
            dst_ref=view(origin, c),
            send_sem=send.at[0, 0],
            recv_sem=sem.at[origin],
            device_id=twin,
            device_id_type=MESH,
        )

    def forward(idx, view, send, recv, twin_recv):
        origin = place(idx)[0]

        @pl.when(idx > 0)
        def _():
            arrival(view, origin, core, send, recv).wait_recv()

        for wanted, copy in links(idx, view, send, recv, twin_recv):
            copy.start() if wanted is None else pl.when(wanted)(copy.start)

    def finish(idx, view, send, recv, twin_recv):
        for wanted, copy in links(idx, view, send, recv, twin_recv):
            copy.wait_send() if wanted is None else pl.when(wanted)(copy.wait_send)

    def t_view(origin, c):
        return tbuf.at[origin, c]

    def q_view(origin, c):
        return qbuf.at[c, origin]

    t_all = (t_view, t_send, t_recv, ts_recv)
    q_all = (q_view, q_send, q_recv, qs_recv)

    own_q = pltpu.make_async_copy(basis_ref, qbuf.at[core, me], own_sem.at[0])
    own_t = pltpu.make_async_copy(tok_ref, tbuf.at[me, core], own_sem.at[1])
    own_g = pltpu.make_async_copy(gate_ref, wbuf.at[0], own_sem.at[3])
    own_u = pltpu.make_async_copy(up_ref, wbuf.at[1], own_sem.at[4])
    own_q.start()
    own_t.start()
    own_g.start()
    own_u.start()

    def project(chip):
        total = None
        for h in (0, 1):
            block = qbuf[h, chip]
            twice = jnp.concatenate([block, block], axis=0)
            term = lax.dot_general(
                grad_ref[:, h * half : (h + 1) * half],
                twice,
                (((1,), (1,)), ((), ())),
                preferred_element_type=jnp.float32,
            )
            total = term if total is None else total + term
        named = jnp.where(route_ref[...] == chip, weight_ref[...], 0.0)
        column = jnp.sum(named, axis=1, keepdims=True)
        rmsg[chip, :rows] = (total * column).astype(jnp.bfloat16)
        rmsg[chip, rows:] = aux_ref[...]

    def r_copy(chip):
        return pltpu.make_async_remote_copy(
            src_ref=rmsg.at[chip],
            dst_ref=rbuf.at[core, me],
            send_sem=r_send.at[chip],
            recv_sem=r_recv.at[me],
            device_id=(group, chip // 2, (chip % 2) * 2 + core),
            device_id_type=MESH,
        )

    own_r = pltpu.make_async_copy(rmsg.at[me], rbuf.at[core, me], own_sem.at[2])

    def compute(origin):
        feats = tbuf[origin].reshape(2 * rows, tok_ref.shape[1])
        gate, upper = (
            lax.dot_general(
                wbuf[w], feats, (((1,), (1,)), ((), ())), preferred_element_type=jnp.float32
            )
            for w in (0, 1)
        )
        hidden = (gate / (1.0 + jnp.exp(-gate)) * upper).astype(jnp.bfloat16)
        left = jnp.dot(hid_ref[...], hidden, preferred_element_type=jnp.float32)
        high = left.astype(jnp.bfloat16)
        low = (left - high.astype(jnp.float32)).astype(jnp.bfloat16)
        lbuf[origin, :rank] = high
        lbuf[origin, rank:] = low

    share = pltpu.make_async_remote_copy(
        src_ref=rbuf.at[core],
        dst_ref=rbuf.at[core],
        send_sem=rs_sem.at[0],
        recv_sem=rs_sem.at[1],
        device_id=twin,
        device_id_type=MESH,
    )

    def q_step(idx):
        pl.when(idx < chips)(lambda: forward(idx, *q_all))

        @pl.when((idx >= lag) & (idx < chips + lag))
        def _():
            chip = place(idx - lag)[0]
            arrival(q_view, chip, 1 - core, q_send, qs_recv).wait_recv()
            project(chip)
            pl.when(chip == me)(own_r.start)
            pl.when(chip != me)(lambda: r_copy(chip).start())

    lag = 2
    own_q.wait()
    forward(0, *q_all)
    own_t.wait()
    forward(0, *t_all)
    forward(1, *q_all)
    own_g.wait()
    own_u.wait()

    @pl.loop(1, chips + lag)
    def _(idx):
        q_step(2 * idx)
        q_step(2 * idx + 1)
        pl.when(idx < chips)(lambda: forward(idx, *t_all))

        @pl.when(idx >= lag)
        def _():
            origin = place(idx - lag)[0]
            arrival(t_view, origin, 1 - core, t_send, ts_recv).wait_recv()
            compute(origin)

        @pl.when(idx == chips - 2)
        def _():
            own_r.wait()

            @pl.loop(1, chips)
            def _(step):
                chip = (me + step) % chips
                pltpu.make_async_remote_copy(
                    src_ref=rmsg.at[chip],
                    dst_ref=rbuf.at[core, chip],
                    send_sem=r_send.at[chip],
                    recv_sem=r_recv.at[chip],
                    device_id=twin,
                    device_id_type=MESH,
                ).wait_recv()

            share.start()

    share.wait_recv()
    acc[...] = jnp.zeros_like(acc)

    @pl.loop(0, chips)
    def _(chip):
        token = lax.broadcasted_iota(jnp.int32, (rows, 2 * rank), 0).astype(jnp.float32)
        parts = []
        for c in (0, 1):
            right = rbuf[c, chip, :rows].astype(jnp.float32)
            bounds = rbuf[c, chip, rows:].astype(jnp.float32)
            cols = []
            for p in range(pairs):
                inside = (token >= bounds[p : p + 1]) & (token < bounds[pairs + p : pairs + p + 1])
                cols.append(jnp.where(inside, right, 0.0).astype(jnp.bfloat16))
            parts.append(jnp.concatenate(cols, axis=1))
        spread = jnp.concatenate(parts, axis=0)
        acc[...] += jnp.dot(lbuf[chip], spread, preferred_element_type=jnp.float32)

    width = 2 * rank
    for p in range(pairs):
        cut = slice(p * width, (p + 1) * width)
        fsend[p] = acc[:rank, cut] + acc[rank:, cut]
    fbuf[spot] = fsend[spot]

    def f_copy(step, source):
        peer = (spot + step) % pairs
        return pltpu.make_async_remote_copy(
            src_ref=fsend.at[peer],
            dst_ref=fbuf.at[peer if source else spot],
            send_sem=f_send.at[peer],
            recv_sem=f_recv.at[peer if source else spot],
            device_id=(group, node, peer),
            device_id_type=MESH,
        )

    for step in range(1, pairs):
        f_copy(step, False).start()
    for step in range(1, pairs):
        f_copy(step, True).wait_recv()
    for e in range(pairs // 2):
        pair = fbuf[2 * e] + fbuf[2 * e + 1]
        out_ref[e, 0] = pair[:, :rank]
        out_ref[e, 1] = pair[:, rank:]

    for step in range(1, pairs):
        f_copy(step, False).wait_send()
    share.wait_send()

    @pl.loop(1, chips)
    def _(step):
        r_copy((me + step) % chips).wait_send()

    @pl.loop(0, chips)
    def _(idx):
        finish(idx, *q_all)
        finish(idx, *t_all)


def fused_local(
    tokens,
    out_grad,
    routes,
    route_weight,
    example_id,
    gate_weight,
    up_weight,
    hidden_basis,
    model_basis,
):
    local_count = lax.axis_size("local")
    chips = lax.axis_size("node") * local_count // 2
    examples = 2 * local_count
    rows, width = tokens.shape
    half_width = hidden_basis.shape[1]
    rank = hidden_basis.shape[2]
    before = jnp.sum(
        example_id[None, :] < jnp.arange(examples + 1, dtype=jnp.int32)[:, None], axis=1
    )
    low = jnp.repeat(before[:-1], rank).reshape(local_count, 2 * rank)
    high = jnp.repeat(before[1:], rank).reshape(local_count, 2 * rank)
    fill = jnp.zeros((16 - 2 * local_count, 2 * rank), low.dtype)
    aux = jnp.concatenate([low, high, fill]).astype(jnp.bfloat16)
    vmem = pl.BlockSpec(memory_space=pltpu.VMEM)
    dma = pltpu.SemaphoreType.DMA
    bf16, f32 = jnp.bfloat16, jnp.float32
    flops = 2 * 2 * rows * chips * width * 2 * half_width
    return pl.pallas_call(
        fused_kernel,
        out_shape=jax.ShapeDtypeStruct((local_count // 2, 2, rank, rank), f32),
        in_specs=[vmem] * 5 + [pl.BlockSpec(memory_space=pl.ANY)] * 2 + [vmem] * 2,
        out_specs=vmem,
        scratch_shapes=[
            pltpu.VMEM((2, half_width, width), bf16),
            pltpu.VMEM((chips, 2, rows, width), bf16),
            pltpu.VMEM((2, chips, rank, width // 2), bf16),
            pltpu.VMEM((chips, rows + 16, 2 * rank), bf16),
            pltpu.VMEM((2, chips, rows + 16, 2 * rank), bf16),
            pltpu.VMEM((chips, 2 * rank, 2 * rows), bf16),
            pltpu.VMEM((2 * rank, examples * rank), f32),
            pltpu.VMEM((local_count, rank, 2 * rank), f32),
            pltpu.VMEM((local_count, rank, 2 * rank), f32),
            dma((5,)),
            dma((chips, 5)),
            dma((chips,)),
            dma((chips,)),
            dma((chips, 5)),
            dma((chips,)),
            dma((chips,)),
            dma((chips,)),
            dma((chips,)),
            dma((2,)),
            dma((local_count,)),
            dma((local_count,)),
        ],
        compiler_params=pltpu.CompilerParams(
            collective_id=0, has_side_effects=True, vmem_limit_bytes=56 * 1024 * 1024
        ),
        cost_estimate=pl.CostEstimate(flops=flops, bytes_accessed=1 << 23, transcendentals=0),
    )(
        tokens,
        out_grad,
        routes,
        route_weight,
        aux,
        gate_weight[0].T,
        up_weight[0].T,
        hidden_basis[0].T,
        model_basis[0].T,
    )


def solution(mesh):
    sizes = dict(mesh.shape)
    small = sizes["node"] == 8 and sizes["local"] == 4
    body = fused_local if small else local
    in_specs = (
        P(("groups", "node", "local"), None),
        P(("groups", "node", "local"), None),
        P(("groups", "node", "local"), None),
        P(("groups", "node", "local"), None),
        P(("groups", "node", "local")),
        P(("node", "local"), None, None),
        P(("node", "local"), None, None),
        P(("node", "local"), None, None),
        P(("node", "local"), None, None),
    )
    out_specs = P("node", ("groups", "local"), None, None)
    return jax.shard_map(body, mesh=mesh, in_specs=in_specs, out_specs=out_specs, check_vma=False)
```

```python
import functools

import jax
import jax.numpy as jnp
from jax import lax
from jax.experimental import pallas as pl
from jax.experimental.pallas import tpu as pltpu
from jax.sharding import PartitionSpec as P

MESH = pl.DeviceIdType.MESH


def swapped(block, axis, stride):
    count = lax.axis_size(axis)
    route = []
    for low in range(count):
        high = low | 1 << stride
        if high != low and high < count:
            route += [(low, high), (high, low)]
    return lax.ppermute(block, axis, route)


def local(
    tokens,
    out_grad,
    routes,
    route_weight,
    example_id,
    gate_weight,
    up_weight,
    hidden_basis,
    model_basis,
):
    node_count = lax.axis_size("node")
    local_count = lax.axis_size("local")
    experts = node_count * local_count // 2
    per_node = local_count // 2
    tok_rows, model_width = tokens.shape
    top_count = routes.shape[1]
    capacity = 3 * tok_rows * top_count // (2 * experts)
    half_width = model_width // 2
    examples = 2 * local_count
    rank_size = hidden_basis.shape[2]
    flat_routes = routes.reshape(-1)
    expert_ids = jnp.arange(experts, dtype=jnp.int32)
    chosen = (flat_routes[:, None] == expert_ids[None, :]).astype(jnp.int32)
    earlier = jnp.cumsum(chosen, axis=0) - chosen
    placing = jnp.sum(earlier * chosen, axis=1)
    target = flat_routes * capacity + placing
    owner_row = (
        jnp.full((experts * capacity,), -1, jnp.int32)
        .at[target]
        .set(jnp.arange(tok_rows * top_count, dtype=jnp.int32))
    )
    filled = owner_row >= 0
    source = jnp.maximum(owner_row, 0)
    token_of = source // top_count
    weight_of = jnp.where(filled, route_weight.reshape(-1)[source], jnp.zeros((), jnp.float32))
    sent_rows = jnp.where(filled[:, None], tokens[token_of], jnp.zeros((), tokens.dtype))
    sent_grads = (weight_of[:, None] * out_grad[token_of].astype(jnp.float32)).astype(jnp.bfloat16)
    sent_examples = example_id[token_of].astype(jnp.bfloat16)
    grid_feats = jnp.repeat(sent_rows.reshape(experts, capacity, model_width), 2, axis=0)
    grid_grads = (
        sent_grads.reshape(experts, capacity, 2, half_width)
        .transpose(0, 2, 1, 3)
        .reshape(2 * experts, capacity, half_width)
    )
    grid_examples = jnp.repeat(sent_examples.reshape(experts, capacity), 2, axis=0)
    row_feats = lax.all_to_all(
        grid_feats, ("node", "local"), split_axis=0, concat_axis=0, tiled=True
    )
    row_grads = lax.all_to_all(
        grid_grads, ("node", "local"), split_axis=0, concat_axis=0, tiled=True
    )
    row_examples = lax.all_to_all(
        grid_examples, ("node", "local"), split_axis=0, concat_axis=0, tiled=True
    )
    leading = row_feats.shape[:2]
    flat_feats = row_feats.reshape(-1, model_width)
    gate_proj = jnp.dot(flat_feats, gate_weight[0], preferred_element_type=jnp.float32)
    up_proj = jnp.dot(flat_feats, up_weight[0], preferred_element_type=jnp.float32)
    hidden = (jax.nn.silu(gate_proj) * up_proj).astype(jnp.bfloat16)
    left_side = jnp.dot(hidden, hidden_basis[0], preferred_element_type=jnp.float32)
    right_part = jnp.dot(
        row_grads.reshape(-1, half_width), model_basis[0], preferred_element_type=jnp.float32
    )
    left_side, right_part, arrived = (
        left_side.reshape(leading + (rank_size,)),
        right_part.reshape(leading + (rank_size,)),
        row_examples,
    )
    right_side = right_part + swapped(right_part, "local", 0)
    flat_left = left_side.reshape(-1, rank_size)
    flat_right = right_side.reshape(-1, rank_size)
    flat_examples = arrived.reshape(-1).astype(jnp.int32)
    member = (flat_examples[:, None] == jnp.arange(examples, dtype=jnp.int32)[None, :]).astype(
        jnp.float32
    )
    spread = (member[:, :, None] * flat_left[:, None, :]).reshape(
        flat_left.shape[0], examples * rank_size
    )
    logged_own = lax.dot_general(
        spread,
        flat_right,
        (((0,), (0,)), ((), ())),
        precision=lax.Precision.HIGHEST,
        preferred_element_type=jnp.float32,
    ).reshape(examples, rank_size, rank_size)
    slot_in_node = lax.axis_index("local") // 2
    chooser = (jnp.arange(per_node, dtype=jnp.int32) == slot_in_node).astype(jnp.float32)
    padded_term = chooser[:, None, None, None] * logged_own[None]
    return lax.psum_scatter(padded_term, "local", scatter_dimension=1, tiled=True)


def fused_kernel(
    tok_ref,
    grad_ref,
    route_ref,
    weight_ref,
    aux_ref,
    gate_ref,
    up_ref,
    hid_ref,
    basis_ref,
    out_ref,
    wbuf,
    tbuf,
    qbuf,
    rmsg,
    rbuf,
    lbuf,
    acc,
    fsend,
    fbuf,
    own_sem,
    t_send,
    t_recv,
    ts_recv,
    q_send,
    q_recv,
    qs_recv,
    r_send,
    r_recv,
    rs_sem,
    f_send,
    f_recv,
):
    group = lax.axis_index("groups")
    node = lax.axis_index("node")
    spot = lax.axis_index("local")
    depth = lax.axis_size("node") // 2
    chips = 2 * lax.axis_size("node")
    pairs = lax.axis_size("local")
    zi, yi = node // 2, node % 2
    xi, core = spot // 2, spot % 2
    me = node * 2 + xi
    half = grad_ref.shape[1] // 2
    rank = hid_ref.shape[0]
    rows = tok_ref.shape[0]

    def device(z, y, x, c):
        return (group, z * 2 + y, x * 2 + c)

    first_x, first_y = 1 - core, core
    up = device(lax.rem(zi + 1, depth), yi, xi, core)
    down = device(lax.rem(zi + depth - 1, depth), yi, xi, core)
    near = device(zi, (yi + first_y) % 2, (xi + first_x) % 2, core)
    far = device(zi, (yi + first_x) % 2, (xi + first_y) % 2, core)
    twin = device(zi, yi, xi, 1 - core)

    barrier = pltpu.get_barrier_semaphore()

    @pl.loop(1, chips)
    def _(step):
        chip = (me + step) % chips
        pl.semaphore_signal(
            barrier, inc=1, device_id=(group, chip // 2, (chip % 2) * 2 + core), device_id_type=MESH
        )

    for c in (0, 1):
        where = device(zi, yi, (xi + c) % 2, 1 - core)
        pl.semaphore_signal(barrier, inc=1, device_id=where, device_id_type=MESH)
    pl.semaphore_wait(barrier, chips + 1)

    least = jnp.minimum(zi, depth - 1 - zi)
    lean = jnp.where(zi > depth - 1 - zi, -1, 1)

    def place(idx):
        n, pos = idx // 4, idx % 4
        one, two = pos % 2, pos // 2
        swing = ((n + 1) // 2) * (1 - 2 * (n % 2))
        dz = jnp.where(n <= 2 * least, swing, lean * (n - least))
        oz = jnp.clip(zi + dz, 0, depth - 1)
        flip_x = one * first_x + two * first_y
        flip_y = one * first_y + two * first_x
        origin = (oz * 2 + (yi + flip_y) % 2) * 2 + (xi + flip_x) % 2
        return origin, one, two, dz

    def links(idx, view, send, recv, twin_recv):
        origin, one, two, dz = place(idx)
        straight = (one == 0) & (two == 0)
        beside = (one == 1) & (two == 0)
        climb = (straight & (dz <= 0)) | (beside & (dz < 0))
        fall = (straight & (dz >= 0)) | (beside & (dz > 0))
        plan = (
            (climb & (zi < depth - 1), up, recv),
            (fall & (zi > 0), down, recv),
            (two == 0, far, recv),
            (straight & (dz >= -1) & (dz <= 1), near, recv),
            (None, twin, twin_recv),
        )
        for j, (wanted, where, sem) in enumerate(plan):
            copy = pltpu.make_async_remote_copy(
                src_ref=view(origin, core),
                dst_ref=view(origin, core),
                send_sem=send.at[origin, j],
                recv_sem=sem.at[origin],
                device_id=where,
                device_id_type=MESH,
            )
            yield wanted, copy

    def arrival(view, origin, c, send, sem):
        return pltpu.make_async_remote_copy(
            src_ref=view(origin, c),
            dst_ref=view(origin, c),
            send_sem=send.at[0, 0],
            recv_sem=sem.at[origin],
            device_id=twin,
            device_id_type=MESH,
        )

    def forward(idx, view, send, recv, twin_recv):
        origin = place(idx)[0]

        @pl.when(idx > 0)
        def _():
            arrival(view, origin, core, send, recv).wait_recv()

        for wanted, copy in links(idx, view, send, recv, twin_recv):
            copy.start() if wanted is None else pl.when(wanted)(copy.start)

    def finish(idx, view, send, recv, twin_recv):
        for wanted, copy in links(idx, view, send, recv, twin_recv):
            copy.wait_send() if wanted is None else pl.when(wanted)(copy.wait_send)

    def t_view(origin, c):
        return tbuf.at[origin, c]

    def q_view(origin, c):
        return qbuf.at[c, origin]

    t_all = (t_view, t_send, t_recv, ts_recv)
    q_all = (q_view, q_send, q_recv, qs_recv)

    own_q = pltpu.make_async_copy(basis_ref, qbuf.at[core, me], own_sem.at[0])
    own_t = pltpu.make_async_copy(tok_ref, tbuf.at[me, core], own_sem.at[1])
    own_g = pltpu.make_async_copy(gate_ref, wbuf.at[0], own_sem.at[3])
    own_u = pltpu.make_async_copy(up_ref, wbuf.at[1], own_sem.at[4])
    own_q.start()
    own_t.start()
    own_g.start()
    own_u.start()

    def project(chip):
        total = None
        for h in (0, 1):
            block = qbuf[h, chip]
            twice = jnp.concatenate([block, block], axis=0)
            term = lax.dot_general(
                grad_ref[:, h * half : (h + 1) * half],
                twice,
                (((1,), (1,)), ((), ())),
                preferred_element_type=jnp.float32,
            )
            total = term if total is None else total + term
        named = jnp.where(route_ref[...] == chip, weight_ref[...], 0.0)
        column = jnp.sum(named, axis=1, keepdims=True)
        rmsg[chip, :rows] = (total * column).astype(jnp.bfloat16)
        rmsg[chip, rows:] = aux_ref[...]

    def r_copy(chip):
        return pltpu.make_async_remote_copy(
            src_ref=rmsg.at[chip],
            dst_ref=rbuf.at[core, me],
            send_sem=r_send.at[chip],
            recv_sem=r_recv.at[me],
            device_id=(group, chip // 2, (chip % 2) * 2 + core),
            device_id_type=MESH,
        )

    own_r = pltpu.make_async_copy(rmsg.at[me], rbuf.at[core, me], own_sem.at[2])

    def compute(origin):
        feats = tbuf[origin].reshape(2 * rows, tok_ref.shape[1])
        gate, upper = (
            lax.dot_general(
                wbuf[w], feats, (((1,), (1,)), ((), ())), preferred_element_type=jnp.float32
            )
            for w in (0, 1)
        )
        hidden = (gate / (1.0 + jnp.exp(-gate)) * upper).astype(jnp.bfloat16)
        left = jnp.dot(hid_ref[...], hidden, preferred_element_type=jnp.float32)
        high = left.astype(jnp.bfloat16)
        low = (left - high.astype(jnp.float32)).astype(jnp.bfloat16)
        lbuf[origin, :rank] = high
        lbuf[origin, rank:] = low

    share = pltpu.make_async_remote_copy(
        src_ref=rbuf.at[core],
        dst_ref=rbuf.at[core],
        send_sem=rs_sem.at[0],
        recv_sem=rs_sem.at[1],
        device_id=twin,
        device_id_type=MESH,
    )

    def q_step(idx):
        pl.when(idx < chips)(lambda: forward(idx, *q_all))

        @pl.when((idx >= lag) & (idx < chips + lag))
        def _():
            chip = place(idx - lag)[0]
            arrival(q_view, chip, 1 - core, q_send, qs_recv).wait_recv()
            project(chip)
            pl.when(chip == me)(own_r.start)
            pl.when(chip != me)(lambda: r_copy(chip).start())

    lag = 2
    own_q.wait()
    forward(0, *q_all)
    own_t.wait()
    forward(0, *t_all)
    forward(1, *q_all)
    own_g.wait()
    own_u.wait()

    @pl.loop(1, chips + lag)
    def _(idx):
        q_step(2 * idx)
        q_step(2 * idx + 1)
        pl.when(idx < chips)(lambda: forward(idx, *t_all))

        @pl.when(idx >= lag)
        def _():
            origin = place(idx - lag)[0]
            arrival(t_view, origin, 1 - core, t_send, ts_recv).wait_recv()
            compute(origin)

        @pl.when(idx == chips - 2)
        def _():
            own_r.wait()

            @pl.loop(1, chips)
            def _(step):
                chip = (me + step) % chips
                pltpu.make_async_remote_copy(
                    src_ref=rmsg.at[chip],
                    dst_ref=rbuf.at[core, chip],
                    send_sem=r_send.at[chip],
                    recv_sem=r_recv.at[chip],
                    device_id=twin,
                    device_id_type=MESH,
                ).wait_recv()

            share.start()

    share.wait_recv()
    acc[...] = jnp.zeros_like(acc)

    @pl.loop(0, chips)
    def _(chip):
        token = lax.broadcasted_iota(jnp.int32, (rows, 2 * rank), 0).astype(jnp.float32)
        parts = []
        for c in (0, 1):
            right = rbuf[c, chip, :rows].astype(jnp.float32)
            bounds = rbuf[c, chip, rows:].astype(jnp.float32)
            cols = []
            for p in range(pairs):
                inside = (token >= bounds[p : p + 1]) & (token < bounds[pairs + p : pairs + p + 1])
                cols.append(jnp.where(inside, right, 0.0).astype(jnp.bfloat16))
            parts.append(jnp.concatenate(cols, axis=1))
        spread = jnp.concatenate(parts, axis=0)
        acc[...] += jnp.dot(lbuf[chip], spread, preferred_element_type=jnp.float32)

    width = 2 * rank
    for p in range(pairs):
        cut = slice(p * width, (p + 1) * width)
        fsend[p] = acc[:rank, cut] + acc[rank:, cut]
    fbuf[spot] = fsend[spot]

    def f_copy(step, source):
        peer = (spot + step) % pairs
        return pltpu.make_async_remote_copy(
            src_ref=fsend.at[peer],
            dst_ref=fbuf.at[peer if source else spot],
            send_sem=f_send.at[peer],
            recv_sem=f_recv.at[peer if source else spot],
            device_id=(group, node, peer),
            device_id_type=MESH,
        )

    for step in range(1, pairs):
        f_copy(step, False).start()
    for step in range(1, pairs):
        f_copy(step, True).wait_recv()
    for e in range(pairs // 2):
        pair = fbuf[2 * e] + fbuf[2 * e + 1]
        out_ref[e, 0] = pair[:, :rank]
        out_ref[e, 1] = pair[:, rank:]

    for step in range(1, pairs):
        f_copy(step, False).wait_send()
    share.wait_send()

    @pl.loop(1, chips)
    def _(step):
        r_copy((me + step) % chips).wait_send()

    @pl.loop(0, chips)
    def _(idx):
        finish(idx, *q_all)
        finish(idx, *t_all)


def fused_local(
    tokens,
    out_grad,
    routes,
    route_weight,
    example_id,
    gate_weight,
    up_weight,
    hidden_basis,
    model_basis,
):
    local_count = lax.axis_size("local")
    chips = lax.axis_size("node") * local_count // 2
    examples = 2 * local_count
    rows, width = tokens.shape
    half_width = hidden_basis.shape[1]
    rank = hidden_basis.shape[2]
    before = jnp.sum(
        example_id[None, :] < jnp.arange(examples + 1, dtype=jnp.int32)[:, None], axis=1
    )
    low = jnp.repeat(before[:-1], rank).reshape(local_count, 2 * rank)
    high = jnp.repeat(before[1:], rank).reshape(local_count, 2 * rank)
    fill = jnp.zeros((16 - 2 * local_count, 2 * rank), low.dtype)
    aux = jnp.concatenate([low, high, fill]).astype(jnp.bfloat16)
    vmem = pl.BlockSpec(memory_space=pltpu.VMEM)
    dma = pltpu.SemaphoreType.DMA
    bf16, f32 = jnp.bfloat16, jnp.float32
    flops = 2 * 2 * rows * chips * width * 2 * half_width
    return pl.pallas_call(
        fused_kernel,
        out_shape=jax.ShapeDtypeStruct((local_count // 2, 2, rank, rank), f32),
        in_specs=[vmem] * 5 + [pl.BlockSpec(memory_space=pl.ANY)] * 2 + [vmem] * 2,
        out_specs=vmem,
        scratch_shapes=[
            pltpu.VMEM((2, half_width, width), bf16),
            pltpu.VMEM((chips, 2, rows, width), bf16),
            pltpu.VMEM((2, chips, rank, width // 2), bf16),
            pltpu.VMEM((chips, rows + 16, 2 * rank), bf16),
            pltpu.VMEM((2, chips, rows + 16, 2 * rank), bf16),
            pltpu.VMEM((chips, 2 * rank, 2 * rows), bf16),
            pltpu.VMEM((2 * rank, examples * rank), f32),
            pltpu.VMEM((local_count, rank, 2 * rank), f32),
            pltpu.VMEM((local_count, rank, 2 * rank), f32),
            dma((5,)),
            dma((chips, 5)),
            dma((chips,)),
            dma((chips,)),
            dma((chips, 5)),
            dma((chips,)),
            dma((chips,)),
            dma((chips,)),
            dma((chips,)),
            dma((2,)),
            dma((local_count,)),
            dma((local_count,)),
        ],
        compiler_params=pltpu.CompilerParams(
            collective_id=0, has_side_effects=True, vmem_limit_bytes=56 * 1024 * 1024
        ),
        cost_estimate=pl.CostEstimate(flops=flops, bytes_accessed=1 << 23, transcendentals=0),
    )(
        tokens,
        out_grad,
        routes,
        route_weight,
        aux,
        gate_weight[0].T,
        up_weight[0].T,
        hidden_basis[0].T,
        model_basis[0].T,
    )


def solution(mesh):
    sizes = dict(mesh.shape)
    small = sizes["node"] == 8 and sizes["local"] == 4
    body = fused_local if small else local
    in_specs = (
        P(("groups", "node", "local"), None),
        P(("groups", "node", "local"), None),
        P(("groups", "node", "local"), None),
        P(("groups", "node", "local"), None),
        P(("groups", "node", "local")),
        P(("node", "local"), None, None),
        P(("node", "local"), None, None),
        P(("node", "local"), None, None),
        P(("node", "local"), None, None),
    )
    out_specs = P("node", ("groups", "local"), None, None)
    return jax.shard_map(body, mesh=mesh, in_specs=in_specs, out_specs=out_specs, check_vma=False)
```
